512 devices in a mesh: inner: 16 (over x_lo, y), outer: 32 (over z, x_hi, core).
Axes of the slice: x: 4 (x_hi: 2, x_lo: 2; x = x_hi * 2 + x_lo), y: 8, z: 8, core: 2. Of those that a mesh axis runs over, the one named last changes fastest.
Arguments:
- acts: bfloat16 [32, 6144, 4096], P('outer', 'inner'), may hold values from -6 to 6
- grad_out: bfloat16 [32, 6144, 512], P('outer', 'inner'), may hold values from -0.019042969 to 0.019042969
- carried: float32 [32, 4096, 512], P('outer', 'inner'), may hold values from -3 to 3
- start_seed: int32 [], replicated, may hold values from 0 to 999
Outputs:
- update: bfloat16 [4096, 512], P(None, 'outer')
- new_carried: float32 [32, 4096, 512], P('outer', 'inner')
The draws below stay inside these ranges and needn't reach their ends.
All inputs are finite; a program needn't handle non-finite values.
Results may differ from the reference program's by a relative error of at most 0.014.
Values may be sent and summed in bfloat16 or wider, within the bound.
No kernel may reach another device: no remote copies, remote signals or barrier semaphores. Data moves between devices by JAX's collectives and lax.ppermute only.
A program may use at most 64 MiB of HBM per device.

```python
import jax
import jax.numpy as jnp
from jax import lax

D = 4096
KV = 512
RANK = 64
TOK_DEV = 384
GROUP_TOK = 6144
GROUPS = 32
N_INNER = 16
N_OUTER = 32


def block_levels(key, shape, pieces, low, top_value):
    factor_of = 1.0
    for position, blocks in pieces:
        steps = jax.random.uniform(jax.random.fold_in(jax.random.fold_in(key, 6), position), (blocks,), jnp.float32, low / len(pieces), top_value / len(pieces))
        factor_of = factor_of * jnp.repeat(jnp.exp(steps), shape[position] // blocks).reshape((-1,) + (1,) * (len(shape) - 1 - position))
    return factor_of


def bell_draw(stream_key, extent, spread, limit, shards=(), held_as=jnp.bfloat16):
    array = spread * jax.random.normal(stream_key, extent, jnp.float32)
    if shards:
        array = array * block_levels(stream_key, extent, shards, -0.22, 0.18)
    return jnp.clip(array, -limit, limit).astype(held_as)


def setup_inputs(seed: int = 0) -> dict:
    splits = jax.random.split(jax.random.key(seed), 5)
    return {
        "acts": bell_draw(splits[0], (GROUPS, GROUP_TOK, D), 1.0, 6.0, ((0, 32), (1, 16))),
        "grad_out": bell_draw(splits[1], (GROUPS, GROUP_TOK, KV), (0.25 / GROUP_TOK ** 0.5), 0.019042969, ((0, 32), (1, 16))),
        "carried": bell_draw(splits[2], (GROUPS, D, KV), 0.5, 3.0, ((0, 32), (1, 16)), jnp.float32),
        "start_seed": jax.random.randint(splits[3], (), 0, 1000).astype(jnp.int32),
    }


def seeded_start(start_seed):
    index = jnp.arange(KV * RANK, dtype=jnp.int32)
    seed_term = jnp.asarray(start_seed, jnp.int32) * jnp.int32(19349663)
    hashed = index * jnp.int32(73856093) ^ seed_term
    hashed = hashed ^ lax.shift_right_logical(hashed, jnp.int32(13))
    hashed = hashed * jnp.int32(1274126177)
    hashed = hashed ^ lax.shift_right_logical(hashed, jnp.int32(16))
    fraction = (hashed & jnp.int32(16777215)).astype(jnp.float32) / 16777216.0
    return (fraction - 0.5).reshape(KV, RANK)

def group_work(inputs):
    acts_g, grad_g, carried_g = inputs
    blocks_x = acts_g.reshape(N_INNER, TOK_DEV, D)
    blocks_v = grad_g.reshape(N_INNER, TOK_DEV, KV)

    def add_block(total, pair):
        term = jnp.dot(pair[0].T.astype(jnp.float32), pair[1].astype(jnp.float32), preferred_element_type=jnp.float32).astype(jnp.bfloat16)
        term = lax.optimization_barrier(term)
        return (total + term.astype(jnp.float32), None)
    total, unused = lax.scan(add_block, jnp.zeros((D, KV), jnp.float32), (blocks_x, blocks_v))
    return total + carried_g

def reference(acts, grad_out, carried, start_seed):
    work = lax.map(group_work, (acts, grad_out, carried))
    start = seeded_start(start_seed)
    left = jnp.einsum('gdk,kr->dr', work, start, precision=lax.Precision.HIGHEST)
    gram = jnp.dot(left.T, left, precision=lax.Precision.HIGHEST)
    chol = jnp.linalg.cholesky(gram)
    basis = lax.linalg.triangular_solve(chol, left, left_side=False, lower=True, transpose_a=True)
    right = jnp.einsum('gdk,dr->kr', work, basis, precision=lax.Precision.HIGHEST) / N_OUTER
    approx = jnp.dot(basis, right.T, precision=lax.Precision.HIGHEST)
    return (approx.astype(jnp.bfloat16), work - approx[None])
```

```python
import jax
import jax.numpy as jnp
from jax import lax
from jax.sharding import PartitionSpec as P

RANK = 64
HI = lax.Precision.HIGHEST
F32 = jnp.float32
BF16 = jnp.bfloat16


def seeded_start(start_seed, width, rank_size):
    index = jnp.arange(width * rank_size, dtype=jnp.int32)
    seed_term = jnp.asarray(start_seed, jnp.int32) * jnp.int32(19349663)
    hashed = index * jnp.int32(73856093) ^ seed_term
    hashed = hashed ^ lax.shift_right_logical(hashed, jnp.int32(13))
    hashed = hashed * jnp.int32(1274126177)
    hashed = hashed ^ lax.shift_right_logical(hashed, jnp.int32(16))
    fraction = (hashed & jnp.int32(16777215)).astype(jnp.float32) / 16777216.0
    return (fraction - 0.5).reshape(width, rank_size)


def split2(a, axis):
    high = a.astype(BF16)
    low = (a - high.astype(F32)).astype(BF16)
    return jnp.concatenate([high, low], axis)


def spread(piece, count):
    return jnp.broadcast_to(piece[None], (count,) + piece.shape)


def per_device(acts, grad_out, carried, start_seed):
    x, v, c = acts[0], grad_out[0], carried[0]
    tokens, feats = x.shape
    width = v.shape[1]
    rows = c.shape[0]
    n_in, n_out = lax.axis_size("inner"), lax.axis_size("outer")
    inner, outer = lax.axis_index("inner"), lax.axis_index("outer")
    core = outer % 2
    half = rows // 2
    siblings = [(i, i ^ 1) for i in range(n_out)]
    same_core = [[i for i in range(n_out) if i % 2 == k] for k in range(2)]

    partial = lax.dot_general(x, v, (((0,), (0,)), ((), ())), preferred_element_type=F32).astype(BF16)
    grad = lax.psum_scatter(partial, "inner", scatter_dimension=0, tiled=True)

    start = seeded_start(start_seed, width, RANK)
    with jax.named_scope("left_part"):
        vs = jnp.dot(v.astype(F32), start, precision=HI)
        both = lax.dot_general(split2(vs, 1), x, (((0,), (0,)), ((), ())), preferred_element_type=F32)
        left_t = both[:RANK] + both[RANK:]
        own = lax.dot_general(start, c, (((0,), (1,)), ((), ())), precision=HI)
        at = (0, inner * rows)
        left_t = lax.dynamic_update_slice(left_t, lax.dynamic_slice(left_t, at, own.shape) + own, at)
        chunks = left_t.reshape(RANK, n_in, 2, half).transpose(2, 1, 0, 3)
    with jax.named_scope("left_sum"):
        keep = lax.dynamic_index_in_dim(chunks, core, 0, False)
        give = lax.dynamic_index_in_dim(chunks, 1 - core, 0, False)
        pair = keep + lax.ppermute(give, "outer", siblings)
        got = lax.all_to_all(pair.astype(BF16), "inner", 0, 0)
        mine = jnp.sum(got.astype(F32), 0).astype(BF16)
        got = lax.all_to_all(spread(mine, n_out // 2), "outer", 0, 0, axis_index_groups=same_core)
        mine = jnp.sum(got.astype(F32), 0).astype(BF16)
    with jax.named_scope("left_gather"):
        near = lax.all_to_all(spread(mine, n_in), "inner", 0, 0)
        far = lax.ppermute(near, "outer", siblings)
        first = core == 0
        whole = jnp.stack([jnp.where(first, near, far), jnp.where(first, far, near)])
        left_t = whole.transpose(2, 1, 0, 3).reshape(RANK, feats)
        own_t = lax.dynamic_slice(left_t, at, (RANK, rows))
    with jax.named_scope("right_part"):
        y = lax.dot_general(x, left_t, (((1,), (1,)), ((), ())), preferred_element_type=F32)
        both = lax.dot_general(v, split2(y, 1), (((0,), (0,)), ((), ())), preferred_element_type=F32)
        m = both[:, :RANK] + both[:, RANK:]
        m = m + lax.dot_general(c, own_t.astype(F32), (((0,), (1,)), ((), ())), precision=HI)
        packed = jnp.concatenate([m[: width // 2], m[width // 2 :]], 1).reshape(n_out, -1, 2 * RANK)
    with jax.named_scope("right_sum"):
        mine = jnp.sum(lax.all_to_all(packed, "outer", 0, 0), 0)
        mine = jnp.sum(lax.all_to_all(spread(mine, n_in), "inner", 0, 0), 0)
        packed = lax.all_to_all(spread(mine, n_out), "outer", 0, 0).reshape(width // 2, 2 * RANK)
        m = jnp.concatenate([packed[:, :RANK], packed[:, RANK:]], 0)
    with jax.named_scope("factor"):
        gram = lax.dot_general(left_t, left_t, (((1,), (1,)), ((), ())), preferred_element_type=F32)
        chol = jnp.linalg.cholesky(gram)
        inv = lax.linalg.triangular_solve(chol, jnp.eye(RANK, dtype=F32), left_side=True, lower=True)
    with jax.named_scope("result"):
        right_t = lax.dot_general(inv, m, (((1,), (1,)), ((), ())), precision=HI) / n_out
        q = lax.dot_general(inv, right_t, (((0,), (0,)), ((), ())), precision=HI)
        cols = width // n_out
        q_mine = lax.dynamic_slice_in_dim(q, outer * cols, cols, 1)
        update = lax.dot_general(left_t.astype(F32), q_mine, (((0,), (0,)), ((), ())), precision=HI).astype(BF16)
        approx = lax.dot_general(own_t.astype(F32), q, (((0,), (0,)), ((), ())), precision=HI)
        return (update, (grad.astype(F32) + c - approx)[None])


def solution(mesh):
    placed = (P("outer", "inner", None), P("outer", "inner", None), P("outer", "inner", None), P())
    return jax.shard_map(
        per_device,
        mesh=mesh,
        in_specs=placed,
        out_specs=(P(None, "outer"), P("outer", "inner", None)),
        check_vma=False,
    )
```

```python
import functools

import jax
import jax.numpy as jnp
from jax import lax
from jax.experimental import pallas as pl
from jax.experimental.pallas import tpu as pltpu
from jax.sharding import PartitionSpec as P

RANK = 64
LANES = 128
HI = lax.Precision.HIGHEST
F32 = jnp.float32
BF16 = jnp.bfloat16
MIB = 1024 * 1024
CUTS = (20, 42)


def seeded_start_t(seed, width):
    shape = (RANK, width)
    index = lax.broadcasted_iota(jnp.int32, shape, 1) * RANK + lax.broadcasted_iota(jnp.int32, shape, 0)
    hashed = index * jnp.int32(73856093) ^ (seed * jnp.int32(19349663))
    hashed = hashed ^ lax.shift_right_logical(hashed, jnp.int32(13))
    hashed = hashed * jnp.int32(1274126177)
    hashed = hashed ^ lax.shift_right_logical(hashed, jnp.int32(16))
    return (hashed & jnp.int32(16777215)).astype(F32) / 16777216.0 - 0.5


def terms(a, count):
    out = []
    for _ in range(count):
        out.append(a.astype(BF16))
        a = a - out[-1].astype(F32)
    return out


def dot(a, b, dims, **kw):
    return lax.dot_general(a, b, (dims, ((), ())), preferred_element_type=F32, **kw)


NN = ((1,), (0,))
NT = ((1,), (1,))
TN = ((0,), (0,))


def position():
    outer = lax.axis_index("outer")
    return lax.axis_index("inner"), outer, lax.rem(outer, 2)


def in_hbm(a):
    return pltpu.with_memory_space_constraint(a, pltpu.HBM)


def in_vmem(a):
    return pltpu.with_memory_space_constraint(a, pltpu.VMEM)


def fetch(pairs, sems):
    copies = [pltpu.make_async_copy(a, b, sems.at[k]) for k, (a, b) in enumerate(pairs)]
    for copy in copies:
        copy.start()
    return copies


def first_kernel(seed_ref, v_hbm, c_hbm, x_hbm, keep_ref, give_ref, part_hbm, v_ref, c_ref, x_ref, part_ref, in_sems, out_sems):
    inner, _, core = position()
    count, tokens, wide = x_ref.shape
    blocks = [(x_hbm.at[:, pl.ds(j * wide, wide)], x_ref.at[j]) for j in range(count)]
    v_copy, c_copy, *x_copies = fetch([(v_hbm, v_ref), (c_hbm, c_ref)] + blocks, in_sems)
    start_t = seeded_start_t(seed_ref[0], v_ref.shape[1])
    start_3 = jnp.concatenate(terms(start_t, 3), 0)
    v_copy.wait()
    parts = dot(start_3, v_ref[...], NT)
    vs_t = parts[:RANK] + parts[RANK : 2 * RANK] + parts[2 * RANK :]
    v_t = v_ref[...].astype(F32).T.astype(BF16)
    lhs = jnp.concatenate(terms(vs_t, 2) + [v_t], 0)
    c_copy.wait()
    c_2 = terms(c_ref[...], 2)
    cs = dot(start_3, c_2[0], NT) + dot(start_3, c_2[1], NT)
    cs = cs[:RANK] + cs[RANK : 2 * RANK] + cs[2 * RANK :]
    per = wide // (2 * LANES)
    out_copies = []
    for j in range(count):
        x_copies[j].wait()
        both = dot(lhs, x_ref[j], NN)
        left = both[:RANK] + both[RANK : 2 * RANK]
        for n in range(per):
            k = j * per + n
            cols = slice(2 * n * LANES, 2 * (n + 1) * LANES)
            block = left[:, cols] + (inner == k).astype(F32) * cs
            even, odd = block[:, :LANES], block[:, LANES:]
            keep_ref[k] = jnp.where(core == 0, even, odd)
            give_ref[k] = jnp.where(core == 0, odd, even)
            part_ref[k] = both[2 * RANK :, cols].astype(BF16)
        span = pl.ds(j * per, per)
        out_copies += fetch([(part_ref.at[span], part_hbm.at[span])], out_sems.at[pl.ds(j, 1)])
    for copy in out_copies:
        copy.wait()


def first_part(seed, v, c, x, n_in):
    tokens, feats = x.shape
    width = v.shape[1]
    count = 8
    vmem, hbm = pl.BlockSpec(memory_space=pltpu.VMEM), pl.BlockSpec(memory_space=pltpu.HBM)
    out = pltpu.VMEM((n_in, RANK, LANES), F32)
    part = pltpu.HBM((n_in, width, 2 * LANES), BF16)
    return pl.pallas_call(
        first_kernel,
        in_specs=[pl.BlockSpec(memory_space=pltpu.SMEM), hbm, hbm, hbm],
        out_specs=[vmem, vmem, hbm],
        out_shape=[out, out, part],
        scratch_shapes=[
            pltpu.VMEM(v.shape, BF16),
            pltpu.VMEM(c.shape, F32),
            pltpu.VMEM((count, tokens, feats // count), BF16),
            pltpu.VMEM((n_in, width, 2 * LANES), BF16),
            pltpu.SemaphoreType.DMA((count + 2,)),
            pltpu.SemaphoreType.DMA((count,)),
        ],
        compiler_params=pltpu.CompilerParams(vmem_limit_bytes=16 * MIB),
        name="first_part",
    )(seed, in_hbm(v), in_hbm(c), in_hbm(x))


def in_order(core, near, far):
    first = core == 0
    near, far = near.astype(F32), far.astype(F32)
    return jnp.concatenate([jnp.where(first, near, far), jnp.where(first, far, near)], 1).astype(BF16)


def right_kernel(near_ref, far_ref, x_ref, v_hbm, c_hbm, out_ref, aug_ref, v_ref, c_ref, sems):
    inner, _, core = position()
    copies = fetch([(v_hbm, v_ref), (c_hbm, c_ref)], sems)
    y = gram = 0.0
    per = 2
    for k in range(0, near_ref.shape[0], per):
        left = jnp.concatenate([in_order(core, near_ref[k + n], far_ref[k + n]) for n in range(per)], 1)
        y += dot(x_ref[:, 2 * k * LANES : 2 * (k + per) * LANES], left, NT)
        gram += dot(left, left, NT)
    eye = lax.broadcasted_iota(jnp.int32, gram.shape, 0) == lax.broadcasted_iota(jnp.int32, gram.shape, 1)
    aug_ref[...] = jnp.concatenate([gram, eye.astype(F32)], 1)
    y_2 = jnp.concatenate(terms(y.T, 2), 0)
    own = in_order(core, near_ref[inner], far_ref[inner])
    for copy in copies:
        copy.wait()
    both = dot(y_2, v_ref[...], NN)
    m = both[:RANK] + both[RANK:]
    for term in terms(c_ref[...], 2):
        m += dot(own, term, NN)
    high = out_ref.shape[1]
    across = m.shape[1] // LANES
    for k in range(out_ref.shape[0]):
        r, q = divmod(k, across)
        out_ref[k] = m[high * r : high * (r + 1), q * LANES : (q + 1) * LANES].astype(out_ref.dtype)


def right_part(near, far, v, c, x):
    high = 16
    tiles = RANK // high * (v.shape[1] // LANES)
    vmem, hbm = pl.BlockSpec(memory_space=pltpu.VMEM), pl.BlockSpec(memory_space=pltpu.HBM)
    return pl.pallas_call(
        right_kernel,
        in_specs=[vmem, vmem, vmem, hbm, hbm],
        out_specs=[vmem, vmem],
        out_shape=[jax.ShapeDtypeStruct((tiles, high, LANES), BF16), pltpu.VMEM((RANK, 2 * RANK), F32)],
        scratch_shapes=[pltpu.VMEM(v.shape, BF16), pltpu.VMEM(c.shape, F32), pltpu.SemaphoreType.DMA((2,))],
        compiler_params=pltpu.CompilerParams(vmem_limit_bytes=12 * MIB),
        name="right_part",
    )(in_vmem(near), in_vmem(far), x, in_hbm(v), in_hbm(c))


def eliminate(aug, begin, end):
    blocks = [aug[8 * k : 8 * k + 8] for k in range(RANK // 8)]
    below = lax.broadcasted_iota(jnp.int32, blocks[0].shape, 0)
    for j in range(begin, end):
        at, sub = divmod(j, 8)
        row = blocks[at][sub : sub + 1]
        scaled = row / row[:, j : j + 1]
        for k in range(at, len(blocks)):
            taken = blocks[k][:, j : j + 1] * scaled
            blocks[k] = blocks[k] - (jnp.where(below > sub, taken, 0.0) if k == at else taken)
    return jnp.concatenate(blocks, 0)


def more_kernel(begin, end, aug_ref, out_ref):
    aug = eliminate(aug_ref[...], begin, end)
    if end == RANK:
        shape = (RANK, 2 * RANK)
        eye = lax.broadcasted_iota(jnp.int32, shape, 0) == lax.broadcasted_iota(jnp.int32, shape, 1)
        pivots = jnp.sum(jnp.where(eye, aug, 0.0), 1, keepdims=True)
        aug = aug * lax.rsqrt(pivots)
    out_ref[...] = aug


def more_call(begin, end, name, aug):
    vmem = pl.BlockSpec(memory_space=pltpu.VMEM)
    return pl.pallas_call(
        functools.partial(more_kernel, begin, end),
        in_specs=[vmem],
        out_specs=vmem,
        out_shape=pltpu.VMEM(aug.shape, F32),
        compiler_params=pltpu.CompilerParams(vmem_limit_bytes=4 * MIB),
        cost_estimate=pl.CostEstimate(flops=4_000_000, bytes_accessed=2_000_000, transcendentals=0),
        name=name,
    )(aug)


def result_kernel(n_out, tiles_ref, inv_ref, near_ref, far_ref, grad_hbm, c_hbm, update_hbm, new_hbm, update_ref, new_ref, grad_ref, c_ref, in_sems, out_sems):
    copies = fetch([(grad_hbm, grad_ref), (c_hbm, c_ref)], in_sems)
    inner, outer, core = position()
    high = tiles_ref.shape[1]
    across = tiles_ref.shape[0] * high // RANK
    m_t = jnp.concatenate(
        [jnp.concatenate([tiles_ref[r * across + q] for q in range(across)], 1) for r in range(RANK // high)], 0
    ).astype(F32)
    inv = inv_ref[:, RANK:]
    right_t = dot(inv, m_t, NN, precision=HI) / n_out
    q = dot(inv, right_t, TN, precision=HI)
    q_2 = terms(q, 2)
    own = in_order(core, near_ref[inner], far_ref[inner])
    approx = dot(jnp.concatenate([own, own], 0), jnp.concatenate(q_2, 0), TN)
    for copy in copies:
        copy.wait()
    new_ref[...] = grad_ref[...].astype(F32).T + c_ref[...] - approx
    rows = new_ref.shape[0] // 2
    out = [(new_ref.at[pl.ds(k * rows, rows)], new_hbm.at[pl.ds(k * rows, rows)]) for k in range(2)]
    out_copies = fetch(out, out_sems)
    cols = update_ref.shape[0]
    shape = (cols, q.shape[1])
    pick = lax.broadcasted_iota(jnp.int32, shape, 1) == outer * cols + lax.broadcasted_iota(jnp.int32, shape, 0)
    pick = pick.astype(BF16)
    q_mine = jnp.concatenate([dot(pick, term, NT).astype(BF16) for term in q_2], 0)
    for i in range(near_ref.shape[0]):
        both = dot(q_mine, in_order(core, near_ref[i], far_ref[i]), NN)
        update_ref[:, 2 * i * LANES : 2 * (i + 1) * LANES] = (both[:cols] + both[cols:]).astype(BF16)
    out_copies += fetch([(update_ref, update_hbm)], out_sems.at[pl.ds(2, 1)])
    for copy in out_copies:
        copy.wait()


def result(tiles, inv, near, far, grad_t, c, n_out):
    vmem, hbm = pl.BlockSpec(memory_space=pltpu.VMEM), pl.BlockSpec(memory_space=pltpu.HBM)
    update = jax.ShapeDtypeStruct((c.shape[1] // n_out, near.shape[0] * 2 * LANES), BF16)
    return pl.pallas_call(
        functools.partial(result_kernel, n_out),
        in_specs=[vmem] * 4 + [hbm] * 2,
        out_specs=[hbm, hbm],
        out_shape=[update, jax.ShapeDtypeStruct(c.shape, F32)],
        scratch_shapes=[
            pltpu.VMEM(update.shape, BF16),
            pltpu.VMEM(c.shape, F32),
            pltpu.VMEM(grad_t.shape, BF16),
            pltpu.VMEM(c.shape, F32),
            pltpu.SemaphoreType.DMA((2,)),
            pltpu.SemaphoreType.DMA((3,)),
        ],
        compiler_params=pltpu.CompilerParams(vmem_limit_bytes=12 * MIB),
        name="result",
    )(tiles, inv, in_vmem(near), in_vmem(far), in_hbm(grad_t), in_hbm(c))


def spread(piece, count):
    return jnp.broadcast_to(piece[None], (count,) + piece.shape)


def chip_groups(n_in, n_out):
    column, plane = {}, {}
    for i in range(n_in * n_out):
        inner, outer = divmod(i, n_out)
        z, x_hi, core = outer // 4, outer // 2 % 2, outer % 2
        column.setdefault((inner, x_hi), []).append(i)
        plane.setdefault((z, core), []).append(i)
    return list(column.values()), list(plane.values())


def per_device(acts, grad_out, carried, start_seed):
    x, v, c = acts[0], grad_out[0], carried[0]
    n_in, n_out = lax.axis_size("inner"), lax.axis_size("outer")
    siblings = [(i, i ^ 1) for i in range(n_out)]
    same_core = [[i for i in range(n_out) if i % 2 == k] for k in range(2)]

    keep, give, part = first_part(start_seed.reshape(1), v, c, x, n_in)
    with jax.named_scope("left_sum"):
        pair = (keep + lax.ppermute(give, "outer", siblings)).astype(BF16)
        got = lax.all_to_all(pair, "inner", 0, 0)
        mine = jnp.sum(got.astype(F32), 0).astype(BF16)
        part, mine = lax.optimization_barrier((part, mine))
        got = lax.all_to_all(spread(mine, n_out // 2), "outer", 0, 0, axis_index_groups=same_core)
        mine = jnp.sum(got.astype(F32), 0).astype(BF16)
    with jax.named_scope("grad"):
        grad_t = lax.psum_scatter(part.reshape(-1, part.shape[2]), "inner", scatter_dimension=0, tiled=True)
    with jax.named_scope("left_gather"):
        near = lax.all_to_all(spread(mine, n_in), "inner", 0, 0)
        far = lax.ppermute(near, "outer", siblings)
    tiles, aug = right_part(near, far, v, c, x)
    with jax.named_scope("right_sum"):
        both_axes = ("inner", "outer")
        column, plane = chip_groups(n_in, n_out)
        aug = more_call(0, CUTS[0], "factor_a", aug)
        got = lax.all_to_all(tiles, both_axes, 0, 0, axis_index_groups=column)
        mine = jnp.sum(got.astype(F32), 0).astype(BF16)
        aug, mine = lax.optimization_barrier((aug, mine))
        aug = more_call(CUTS[0], CUTS[1], "factor_b", aug)
        got = lax.all_to_all(spread(mine, len(plane[0])), both_axes, 0, 0, axis_index_groups=plane)
        mine = jnp.sum(got.astype(F32), 0).astype(BF16)
        aug, mine = lax.optimization_barrier((aug, mine))
        inv = more_call(CUTS[1], RANK, "factor_c", aug)
        tiles = lax.all_to_all(spread(mine, len(column[0])), both_axes, 0, 0, axis_index_groups=column)
    update_t, new_carried = result(tiles, inv, near, far, grad_t, c, n_out)
    return (update_t.T, new_carried[None])


def solution(mesh):
    placed = (P("outer", "inner", None), P("outer", "inner", None), P("outer", "inner", None), P())
    return jax.shard_map(
        per_device,
        mesh=mesh,
        in_specs=placed,
        out_specs=(P(None, "outer"), P("outer", "inner", None)),
        check_vma=False,
    )
```

```python
import functools

import jax
import jax.numpy as jnp
from jax import lax
from jax.experimental import pallas as pl
from jax.experimental.pallas import tpu as pltpu
from jax.sharding import PartitionSpec as P

RANK = 64
LANES = 128
HI = lax.Precision.HIGHEST
F32 = jnp.float32
BF16 = jnp.bfloat16
MIB = 1024 * 1024


def seeded_start_t(seed, width):
    shape = (RANK, width)
    index = lax.broadcasted_iota(jnp.int32, shape, 1) * RANK + lax.broadcasted_iota(jnp.int32, shape, 0)
    hashed = index * jnp.int32(73856093) ^ (seed * jnp.int32(19349663))
    hashed = hashed ^ lax.shift_right_logical(hashed, jnp.int32(13))
    hashed = hashed * jnp.int32(1274126177)
    hashed = hashed ^ lax.shift_right_logical(hashed, jnp.int32(16))
    return (hashed & jnp.int32(16777215)).astype(F32) / 16777216.0 - 0.5


def terms(a, count):
    out = []
    for _ in range(count):
        out.append(a.astype(BF16))
        a = a - out[-1].astype(F32)
    return out


def dot(a, b, dims, **kw):
    return lax.dot_general(a, b, (dims, ((), ())), preferred_element_type=F32, **kw)


NN = ((1,), (0,))
NT = ((1,), (1,))
TN = ((0,), (0,))


def factor_kernel(gram_ref, out_ref):
    *_, out_ref[...] = elimination(gram_ref[...])


def factor(gram):
    vmem = pl.BlockSpec(memory_space=pltpu.VMEM)
    return pl.pallas_call(
        factor_kernel,
        in_specs=[vmem],
        out_specs=vmem,
        out_shape=pltpu.VMEM((RANK, RANK), F32),
        compiler_params=pltpu.CompilerParams(vmem_limit_bytes=4 * MIB),
        cost_estimate=pl.CostEstimate(flops=4_000_000, bytes_accessed=2_000_000, transcendentals=0),
        name="factor",
    )(gram)


def position():
    outer = lax.axis_index("outer")
    return lax.axis_index("inner"), outer, lax.rem(outer, 2)


def in_hbm(a):
    return pltpu.with_memory_space_constraint(a, pltpu.HBM)


def in_vmem(a):
    return pltpu.with_memory_space_constraint(a, pltpu.VMEM)


def fetch(pairs, sems):
    copies = [pltpu.make_async_copy(a, b, sems.at[k]) for k, (a, b) in enumerate(pairs)]
    for copy in copies:
        copy.start()
    return copies


def first_kernel(seed_ref, v_hbm, c_hbm, x_hbm, keep_ref, give_ref, part_hbm, v_ref, c_ref, x_ref, part_ref, in_sems, out_sems):
    inner, _, core = position()
    count, tokens, wide = x_ref.shape
    blocks = [(x_hbm.at[:, pl.ds(j * wide, wide)], x_ref.at[j]) for j in range(count)]
    v_copy, c_copy, *x_copies = fetch([(v_hbm, v_ref), (c_hbm, c_ref)] + blocks, in_sems)
    start_t = seeded_start_t(seed_ref[0], v_ref.shape[1])
    start_3 = jnp.concatenate(terms(start_t, 3), 0)
    v_copy.wait()
    parts = dot(start_3, v_ref[...], NT)
    vs_t = parts[:RANK] + parts[RANK : 2 * RANK] + parts[2 * RANK :]
    v_t = v_ref[...].astype(F32).T.astype(BF16)
    lhs = jnp.concatenate(terms(vs_t, 2) + [v_t], 0)
    per = wide // (2 * LANES)
    out_copies = []
    for j in range(count):
        x_copies[j].wait()
        both = dot(lhs, x_ref[j], NN)
        left = both[:RANK] + both[RANK : 2 * RANK]
        for n in range(per):
            k = j * per + n
            cols = slice(2 * n * LANES, 2 * (n + 1) * LANES)
            block = left[:, cols]
            even, odd = block[:, :LANES], block[:, LANES:]
            keep_ref[k] = jnp.where(core == 0, even, odd)
            give_ref[k] = jnp.where(core == 0, odd, even)
            part_ref[k] = both[2 * RANK :, cols].astype(BF16)
        span = pl.ds(j * per, per)
        out_copies += fetch([(part_ref.at[span], part_hbm.at[span])], out_sems.at[pl.ds(j, 1)])
    c_copy.wait()
    c_2 = terms(c_ref[...], 2)
    cs = dot(start_3, c_2[0], NT) + dot(start_3, c_2[1], NT)
    cs = cs[:RANK] + cs[RANK : 2 * RANK] + cs[2 * RANK :]
    even, odd = cs[:, :LANES], cs[:, LANES:]
    keep_ref[inner] += jnp.where(core == 0, even, odd)
    give_ref[inner] += jnp.where(core == 0, odd, even)
    for copy in out_copies:
        copy.wait()


def first_part(seed, v, c, x, n_in):
    tokens, feats = x.shape
    width = v.shape[1]
    count = 4
    vmem, hbm = pl.BlockSpec(memory_space=pltpu.VMEM), pl.BlockSpec(memory_space=pltpu.HBM)
    out = pltpu.VMEM((n_in, RANK, LANES), F32)
    part = pltpu.HBM((n_in, width, 2 * LANES), BF16)
    return pl.pallas_call(
        first_kernel,
        in_specs=[pl.BlockSpec(memory_space=pltpu.SMEM), hbm, hbm, hbm],
        out_specs=[vmem, vmem, hbm],
        out_shape=[out, out, part],
        scratch_shapes=[
            pltpu.VMEM(v.shape, BF16),
            pltpu.VMEM(c.shape, F32),
            pltpu.VMEM((count, tokens, feats // count), BF16),
            pltpu.VMEM((n_in, width, 2 * LANES), BF16),
            pltpu.SemaphoreType.DMA((count + 2,)),
            pltpu.SemaphoreType.DMA((count,)),
        ],
        compiler_params=pltpu.CompilerParams(vmem_limit_bytes=16 * MIB),
        name="first_part",
    )(seed, in_hbm(v), in_hbm(c), in_hbm(x))


def in_order(core, near, far):
    first = core == 0
    near, far = near.astype(F32), far.astype(F32)
    return jnp.concatenate([jnp.where(first, near, far), jnp.where(first, far, near)], 1).astype(BF16)


def elimination(gram):
    shape = (RANK, 2 * RANK)
    eye = lax.broadcasted_iota(jnp.int32, shape, 0) == lax.broadcasted_iota(jnp.int32, shape, 1)
    aug = jnp.concatenate([gram, eye[:, :RANK].astype(F32)], 1)
    blocks = [aug[8 * k : 8 * k + 8] for k in range(RANK // 8)]
    tile = blocks[0].shape
    sub = lax.broadcasted_iota(jnp.int32, tile, 0)
    full = lambda a: jnp.broadcast_to(a, tile)
    for j in range(0, RANK, 2):
        at, s = divmod(j, 8)
        row_0, row_1 = full(blocks[at][s : s + 1]), full(blocks[at][s + 1 : s + 2])
        a, b = full(row_0[:, j : j + 1]), full(row_0[:, j + 1 : j + 2])
        c = full(row_1[:, j + 1 : j + 2])
        over_a = 1.0 / a
        ratio = b * over_a
        scaled_0 = row_0 * over_a
        scaled_1 = (row_1 - ratio * row_0) / (c - ratio * b)
        for k in range(at, len(blocks)):
            col_0 = full(blocks[k][:, j : j + 1])
            col_1 = full(blocks[k][:, j + 1 : j + 2]) - col_0 * ratio
            if k == at:
                col_0, col_1 = jnp.where(sub > s, col_0, 0.0), jnp.where(sub > s + 1, col_1, 0.0)
            blocks[k] = blocks[k] - col_0 * scaled_0 - col_1 * scaled_1
        yield None
    aug = jnp.concatenate(blocks, 0)
    pivots = jnp.sum(jnp.where(eye, aug, 0.0), 1, keepdims=True)
    yield aug[:, RANK:] * lax.rsqrt(pivots)


def right_kernel(near_ref, far_ref, x_ref, v_hbm, c_hbm, out_ref, inv_ref, v_ref, c_ref, sems):
    inner, _, core = position()
    copies = fetch([(v_hbm, v_ref), (c_hbm, c_ref)], sems)
    per = 2
    lefts = [
        jnp.concatenate([in_order(core, near_ref[k + n], far_ref[k + n]) for n in range(per)], 1)
        for k in range(0, near_ref.shape[0], per)
    ]
    gram = 0.0
    for left in lefts:
        gram += dot(left, left, NT)
    for copy in copies:
        copy.wait()
    y = 0.0
    for k, left in enumerate(lefts):
        y += dot(x_ref[:, 2 * k * per * LANES : 2 * (k + 1) * per * LANES], left, NT)
    y_2 = jnp.concatenate(terms(y.T, 2), 0)
    own = in_order(core, near_ref[inner], far_ref[inner])
    both = dot(y_2, v_ref[...], NN)
    m = both[:RANK] + both[RANK:]
    for term in terms(c_ref[...], 2):
        m += dot(own, term, NN)
    inv_ref[...] = gram
    high = out_ref.shape[1]
    across = m.shape[1] // LANES
    for k in range(out_ref.shape[0]):
        r, q = divmod(k, across)
        out_ref[k] = m[high * r : high * (r + 1), q * LANES : (q + 1) * LANES].astype(out_ref.dtype)


def right_part(near, far, v, c, x):
    high = 16
    tiles = RANK // high * (v.shape[1] // LANES)
    vmem, hbm = pl.BlockSpec(memory_space=pltpu.VMEM), pl.BlockSpec(memory_space=pltpu.HBM)
    return pl.pallas_call(
        right_kernel,
        in_specs=[vmem, vmem, vmem, hbm, hbm],
        out_specs=[vmem, vmem],
        out_shape=[jax.ShapeDtypeStruct((tiles, high, LANES), BF16), pltpu.VMEM((RANK, RANK), F32)],
        scratch_shapes=[pltpu.VMEM(v.shape, BF16), pltpu.VMEM(c.shape, F32), pltpu.SemaphoreType.DMA((2,))],
        compiler_params=pltpu.CompilerParams(vmem_limit_bytes=12 * MIB),
        name="right_part",
    )(in_vmem(near), in_vmem(far), x, in_hbm(v), in_hbm(c))


def result_kernel(n_out, tiles_ref, inv_ref, near_ref, far_hbm, grad_hbm, c_hbm, update_hbm, new_hbm, update_ref, new_ref, far_ref, grad_ref, c_ref, in_sems, out_sems):
    copies = fetch([(far_hbm, far_ref), (grad_hbm, grad_ref), (c_hbm, c_ref)], in_sems)
    inner, outer, core = position()
    high = tiles_ref.shape[1]
    across = tiles_ref.shape[0] * high // RANK
    m_t = jnp.concatenate(
        [jnp.concatenate([tiles_ref[r * across + q] for q in range(across)], 1) for r in range(RANK // high)], 0
    ).astype(F32)
    inv = inv_ref[...]
    right_t = dot(inv, m_t, NN, precision=HI) / n_out
    q = dot(inv, right_t, TN, precision=HI)
    q_2 = terms(q, 2)
    copies[0].wait()
    own = in_order(core, near_ref[inner], far_ref[inner])
    approx = dot(jnp.concatenate([own, own], 0), jnp.concatenate(q_2, 0), TN)
    copies[1].wait()
    copies[2].wait()
    new_ref[...] = grad_ref[...].astype(F32).T + c_ref[...] - approx
    rows = new_ref.shape[0] // 2
    out = [(new_ref.at[pl.ds(k * rows, rows)], new_hbm.at[pl.ds(k * rows, rows)]) for k in range(2)]
    out_copies = fetch(out, out_sems)
    cols = update_ref.shape[0]
    shape = (cols, q.shape[1])
    pick = lax.broadcasted_iota(jnp.int32, shape, 1) == outer * cols + lax.broadcasted_iota(jnp.int32, shape, 0)
    pick = pick.astype(BF16)
    q_mine = jnp.concatenate([dot(pick, term, NT).astype(BF16) for term in q_2], 0)
    for i in range(near_ref.shape[0]):
        both = dot(q_mine, in_order(core, near_ref[i], far_ref[i]), NN)
        update_ref[:, 2 * i * LANES : 2 * (i + 1) * LANES] = (both[:cols] + both[cols:]).astype(BF16)
    out_copies += fetch([(update_ref, update_hbm)], out_sems.at[pl.ds(2, 1)])
    for copy in out_copies:
        copy.wait()


def result(tiles, inv, near, far, grad_t, c, n_out):
    vmem, hbm = pl.BlockSpec(memory_space=pltpu.VMEM), pl.BlockSpec(memory_space=pltpu.HBM)
    update = jax.ShapeDtypeStruct((c.shape[1] // n_out, near.shape[0] * 2 * LANES), BF16)
    return pl.pallas_call(
        functools.partial(result_kernel, n_out),
        in_specs=[vmem] * 3 + [hbm] * 3,
        out_specs=[hbm, hbm],
        out_shape=[update, jax.ShapeDtypeStruct(c.shape, F32)],
        scratch_shapes=[
            pltpu.VMEM(update.shape, BF16),
            pltpu.VMEM(c.shape, F32),
            pltpu.VMEM(far.shape, BF16),
            pltpu.VMEM(grad_t.shape, BF16),
            pltpu.VMEM(c.shape, F32),
            pltpu.SemaphoreType.DMA((3,)),
            pltpu.SemaphoreType.DMA((3,)),
        ],
        compiler_params=pltpu.CompilerParams(vmem_limit_bytes=12 * MIB),
        name="result",
    )(tiles, inv, in_vmem(near), in_hbm(far), in_hbm(grad_t), in_hbm(c))


def spread(piece, count):
    return jnp.broadcast_to(piece[None], (count,) + piece.shape)


def chip_groups(n_in, n_out):
    column, plane = {}, {}
    for i in range(n_in * n_out):
        inner, outer = divmod(i, n_out)
        z, x_hi, core = outer // 4, outer // 2 % 2, outer % 2
        column.setdefault((inner, x_hi), []).append(i)
        plane.setdefault((z, core), []).append(i)
    return list(column.values()), list(plane.values())


def per_device(acts, grad_out, carried, start_seed):
    x, v, c = acts[0], grad_out[0], carried[0]
    n_in, n_out = lax.axis_size("inner"), lax.axis_size("outer")
    siblings = [(i, i ^ 1) for i in range(n_out)]
    same_core = [[i for i in range(n_out) if i % 2 == k] for k in range(2)]

    keep, give, part = first_part(start_seed.reshape(1), v, c, x, n_in)
    with jax.named_scope("left_sum"):
        pair = (keep + lax.ppermute(give, "outer", siblings)).astype(BF16)
        got = lax.all_to_all(pair, "inner", 0, 0)
        mine = jnp.sum(got.astype(F32), 0).astype(BF16)
        part, mine = lax.optimization_barrier((part, mine))
        got = lax.all_to_all(spread(mine, n_out // 2), "outer", 0, 0, axis_index_groups=same_core)
        mine = jnp.sum(got.astype(F32), 0).astype(BF16)
    with jax.named_scope("grad"):
        grad_t = lax.psum_scatter(part.reshape(-1, part.shape[2]), "inner", scatter_dimension=0, tiled=True)
    with jax.named_scope("left_gather"):
        near = lax.all_to_all(spread(mine, n_in), "inner", 0, 0)
        far = lax.ppermute(near, "outer", siblings)
    tiles, inv = right_part(near, far, v, c, x)
    inv = factor(inv)
    with jax.named_scope("right_sum"):
        both_axes = ("inner", "outer")
        column, plane = chip_groups(n_in, n_out)
        got = lax.all_to_all(tiles, both_axes, 0, 0, axis_index_groups=column)
        mine = jnp.sum(got.astype(F32), 0).astype(BF16)
        got = lax.all_to_all(spread(mine, len(plane[0])), both_axes, 0, 0, axis_index_groups=plane)
        mine = jnp.sum(got.astype(F32), 0).astype(BF16)
        tiles = lax.all_to_all(spread(mine, len(column[0])), both_axes, 0, 0, axis_index_groups=column)
    update_t, new_carried = result(tiles, inv, near, far, grad_t, c, n_out)
    return (update_t.T, new_carried[None])


def solution(mesh):
    placed = (P("outer", "inner", None), P("outer", "inner", None), P("outer", "inner", None), P())
    return jax.shard_map(
        per_device,
        mesh=mesh,
        in_specs=placed,
        out_specs=(P(None, "outer"), P("outer", "inner", None)),
        check_vma=False,
    )
```

```python
import functools

import jax
import jax.numpy as jnp
from jax import lax
from jax.experimental import pallas as pl
from jax.experimental.pallas import tpu as pltpu
from jax.sharding import PartitionSpec as P

RANK = 64
LANES = 128
HI = lax.Precision.HIGHEST
F32 = jnp.float32
BF16 = jnp.bfloat16
MIB = 1024 * 1024


def seeded_start_t(seed, width):
    shape = (RANK, width)
    index = lax.broadcasted_iota(jnp.int32, shape, 1) * RANK + lax.broadcasted_iota(jnp.int32, shape, 0)
    hashed = index * jnp.int32(73856093) ^ (seed * jnp.int32(19349663))
    hashed = hashed ^ lax.shift_right_logical(hashed, jnp.int32(13))
    hashed = hashed * jnp.int32(1274126177)
    hashed = hashed ^ lax.shift_right_logical(hashed, jnp.int32(16))
    return (hashed & jnp.int32(16777215)).astype(F32) / 16777216.0 - 0.5


def terms(a, count):
    out = []
    for _ in range(count):
        out.append(a.astype(BF16))
        a = a - out[-1].astype(F32)
    return out


def dot(a, b, dims, **kw):
    return lax.dot_general(a, b, (dims, ((), ())), preferred_element_type=F32, **kw)


NN = ((1,), (0,))
NT = ((1,), (1,))
TN = ((0,), (0,))


def factor_kernel(gram_ref, out_ref):
    *_, out_ref[...] = elimination(gram_ref[...])


def factor(gram):
    vmem = pl.BlockSpec(memory_space=pltpu.VMEM)
    return pl.pallas_call(
        factor_kernel,
        in_specs=[vmem],
        out_specs=vmem,
        out_shape=pltpu.VMEM((RANK, RANK), F32),
        compiler_params=pltpu.CompilerParams(vmem_limit_bytes=4 * MIB),
        cost_estimate=pl.CostEstimate(flops=4_000_000, bytes_accessed=2_000_000, transcendentals=0),
        name="factor",
    )(gram)


def position():
    outer = lax.axis_index("outer")
    return lax.axis_index("inner"), outer, lax.rem(outer, 2)


def in_hbm(a):
    return pltpu.with_memory_space_constraint(a, pltpu.HBM)


def in_vmem(a):
    return pltpu.with_memory_space_constraint(a, pltpu.VMEM)


def fetch(pairs, sems):
    copies = [pltpu.make_async_copy(a, b, sems.at[k]) for k, (a, b) in enumerate(pairs)]
    for copy in copies:
        copy.start()
    return copies


def first_kernel(seed_ref, v_hbm, c_hbm, x_hbm, keep_ref, give_ref, part_hbm, v_ref, c_ref, x_ref, part_ref, in_sems, out_sems):
    inner, _, core = position()
    count, tokens, wide = x_ref.shape
    blocks = [(x_hbm.at[:, pl.ds(j * wide, wide)], x_ref.at[j]) for j in range(count)]
    v_copy, c_copy, *x_copies = fetch([(v_hbm, v_ref), (c_hbm, c_ref)] + blocks, in_sems)
    start_t = seeded_start_t(seed_ref[0], v_ref.shape[1])
    start_3 = jnp.concatenate(terms(start_t, 3), 0)
    v_copy.wait()
    parts = dot(start_3, v_ref[...], NT)
    vs_t = parts[:RANK] + parts[RANK : 2 * RANK] + parts[2 * RANK :]
    v_t = v_ref[...].astype(F32).T.astype(BF16)
    lhs = jnp.concatenate(terms(vs_t, 2) + [v_t], 0)
    per = wide // (2 * LANES)
    out_copies = []
    for j in range(count):
        x_copies[j].wait()
        both = dot(lhs, x_ref[j], NN)
        left = both[:RANK] + both[RANK : 2 * RANK]
        for n in range(per):
            k = j * per + n
            cols = slice(2 * n * LANES, 2 * (n + 1) * LANES)
            block = left[:, cols]
            even, odd = block[:, :LANES], block[:, LANES:]
            keep_ref[k] = jnp.where(core == 0, even, odd)
            give_ref[k] = jnp.where(core == 0, odd, even)
            part_ref[k] = both[2 * RANK :, cols].astype(BF16)
        span = pl.ds(j * per, per)
        out_copies += fetch([(part_ref.at[span], part_hbm.at[span])], out_sems.at[pl.ds(j, 1)])
    c_copy.wait()
    c_2 = terms(c_ref[...], 2)
    cs = dot(start_3, c_2[0], NT) + dot(start_3, c_2[1], NT)
    cs = cs[:RANK] + cs[RANK : 2 * RANK] + cs[2 * RANK :]
    even, odd = cs[:, :LANES], cs[:, LANES:]
    keep_ref[inner] += jnp.where(core == 0, even, odd)
    give_ref[inner] += jnp.where(core == 0, odd, even)
    for copy in out_copies:
        copy.wait()


def first_part(seed, v, c, x, n_in):
    tokens, feats = x.shape
    width = v.shape[1]
    count = 4
    vmem, hbm = pl.BlockSpec(memory_space=pltpu.VMEM), pl.BlockSpec(memory_space=pltpu.HBM)
    out = pltpu.VMEM((n_in, RANK, LANES), F32)
    part = pltpu.HBM((n_in, width, 2 * LANES), BF16)
    return pl.pallas_call(
        first_kernel,
        in_specs=[pl.BlockSpec(memory_space=pltpu.SMEM), hbm, hbm, hbm],
        out_specs=[vmem, vmem, hbm],
        out_shape=[out, out, part],
        scratch_shapes=[
            pltpu.VMEM(v.shape, BF16),
            pltpu.VMEM(c.shape, F32),
            pltpu.VMEM((count, tokens, feats // count), BF16),
            pltpu.VMEM((n_in, width, 2 * LANES), BF16),
            pltpu.SemaphoreType.DMA((count + 2,)),
            pltpu.SemaphoreType.DMA((count,)),
        ],
        compiler_params=pltpu.CompilerParams(vmem_limit_bytes=16 * MIB),
        name="first_part",
    )(seed, in_hbm(v), in_hbm(c), in_hbm(x))


def in_order(core, near, far):
    first = core == 0
    near, far = near.astype(F32), far.astype(F32)
    return jnp.concatenate([jnp.where(first, near, far), jnp.where(first, far, near)], 1).astype(BF16)


def elimination(gram):
    shape = (RANK, 2 * RANK)
    eye = lax.broadcasted_iota(jnp.int32, shape, 0) == lax.broadcasted_iota(jnp.int32, shape, 1)
    aug = jnp.concatenate([gram, eye[:, :RANK].astype(F32)], 1)
    blocks = [aug[8 * k : 8 * k + 8] for k in range(RANK // 8)]
    tile = blocks[0].shape
    sub = lax.broadcasted_iota(jnp.int32, tile, 0)
    full = lambda a: jnp.broadcast_to(a, tile)
    for j in range(0, RANK, 2):
        at, s = divmod(j, 8)
        row_0, row_1 = full(blocks[at][s : s + 1]), full(blocks[at][s + 1 : s + 2])
        a, b = full(row_0[:, j : j + 1]), full(row_0[:, j + 1 : j + 2])
        c = full(row_1[:, j + 1 : j + 2])
        over_a = 1.0 / a
        ratio = b * over_a
        scaled_0 = row_0 * over_a
        scaled_1 = (row_1 - ratio * row_0) / (c - ratio * b)
        for k in range(at, len(blocks)):
            col_0 = full(blocks[k][:, j : j + 1])
            col_1 = full(blocks[k][:, j + 1 : j + 2]) - col_0 * ratio
            if k == at:
                col_0, col_1 = jnp.where(sub > s, col_0, 0.0), jnp.where(sub > s + 1, col_1, 0.0)
            blocks[k] = blocks[k] - col_0 * scaled_0 - col_1 * scaled_1
        yield None
    aug = jnp.concatenate(blocks, 0)
    pivots = jnp.sum(jnp.where(eye, aug, 0.0), 1, keepdims=True)
    yield aug[:, RANK:] * lax.rsqrt(pivots)


def right_kernel(near_ref, far_ref, x_ref, v_hbm, c_hbm, out_ref, inv_ref, v_ref, c_ref, sems):
    inner, _, core = position()
    copies = fetch([(v_hbm, v_ref), (c_hbm, c_ref)], sems)
    per = 2
    lefts = [
        jnp.concatenate([in_order(core, near_ref[k + n], far_ref[k + n]) for n in range(per)], 1)
        for k in range(0, near_ref.shape[0], per)
    ]
    gram = 0.0
    for left in lefts:
        gram += dot(left, left, NT)
    for copy in copies:
        copy.wait()
    y = 0.0
    for k, left in enumerate(lefts):
        y += dot(x_ref[:, 2 * k * per * LANES : 2 * (k + 1) * per * LANES], left, NT)
    y_2 = jnp.concatenate(terms(y.T, 2), 0)
    own = in_order(core, near_ref[inner], far_ref[inner])
    both = dot(y_2, v_ref[...], NN)
    m = both[:RANK] + both[RANK:]
    for term in terms(c_ref[...], 2):
        m += dot(own, term, NN)
    inv_ref[...] = gram
    high = out_ref.shape[1]
    across = m.shape[1] // LANES
    for k in range(out_ref.shape[0]):
        r, q = divmod(k, across)
        out_ref[k] = m[high * r : high * (r + 1), q * LANES : (q + 1) * LANES].astype(out_ref.dtype)


def right_part(near, far, v, c, x):
    high = 16
    tiles = RANK // high * (v.shape[1] // LANES)
    vmem, hbm = pl.BlockSpec(memory_space=pltpu.VMEM), pl.BlockSpec(memory_space=pltpu.HBM)
    return pl.pallas_call(
        right_kernel,
        in_specs=[vmem, vmem, vmem, hbm, hbm],
        out_specs=[vmem, vmem],
        out_shape=[jax.ShapeDtypeStruct((tiles, high, LANES), BF16), pltpu.VMEM((RANK, RANK), F32)],
        scratch_shapes=[pltpu.VMEM(v.shape, BF16), pltpu.VMEM(c.shape, F32), pltpu.SemaphoreType.DMA((2,))],
        compiler_params=pltpu.CompilerParams(vmem_limit_bytes=12 * MIB),
        name="right_part",
    )(in_vmem(near), in_vmem(far), x, in_hbm(v), in_hbm(c))


def result_kernel(n_out, tiles_ref, inv_ref, near_ref, far_hbm, grad_hbm, c_hbm, update_hbm, new_hbm, update_ref, new_ref, far_ref, grad_ref, c_ref, in_sems, out_sems):
    copies = fetch([(far_hbm, far_ref), (grad_hbm, grad_ref), (c_hbm, c_ref)], in_sems)
    inner, outer, core = position()
    high = tiles_ref.shape[1]
    across = tiles_ref.shape[0] * high // RANK
    m_t = jnp.concatenate(
        [jnp.concatenate([tiles_ref[r * across + q] for q in range(across)], 1) for r in range(RANK // high)], 0
    ).astype(F32)
    inv = inv_ref[...]
    right_t = dot(inv, m_t, NN, precision=HI) / n_out
    q = dot(inv, right_t, TN, precision=HI)
    q_2 = terms(q, 2)
    copies[0].wait()
    own = in_order(core, near_ref[inner], far_ref[inner])
    approx = dot(jnp.concatenate([own, own], 0), jnp.concatenate(q_2, 0), TN)
    copies[1].wait()
    copies[2].wait()
    new_ref[...] = grad_ref[...].astype(F32).T + c_ref[...] - approx
    rows = new_ref.shape[0] // 2
    out = [(new_ref.at[pl.ds(k * rows, rows)], new_hbm.at[pl.ds(k * rows, rows)]) for k in range(2)]
    out_copies = fetch(out, out_sems)
    cols = update_ref.shape[0]
    shape = (cols, q.shape[1])
    pick = lax.broadcasted_iota(jnp.int32, shape, 1) == outer * cols + lax.broadcasted_iota(jnp.int32, shape, 0)
    pick = pick.astype(BF16)
    q_mine = jnp.concatenate([dot(pick, term, NT).astype(BF16) for term in q_2], 0)
    for i in range(near_ref.shape[0]):
        both = dot(q_mine, in_order(core, near_ref[i], far_ref[i]), NN)
        update_ref[:, 2 * i * LANES : 2 * (i + 1) * LANES] = (both[:cols] + both[cols:]).astype(BF16)
    out_copies += fetch([(update_ref, update_hbm)], out_sems.at[pl.ds(2, 1)])
    for copy in out_copies:
        copy.wait()


def result(tiles, inv, near, far, grad_t, c, n_out):
    vmem, hbm = pl.BlockSpec(memory_space=pltpu.VMEM), pl.BlockSpec(memory_space=pltpu.HBM)
    update = jax.ShapeDtypeStruct((c.shape[1] // n_out, near.shape[0] * 2 * LANES), BF16)
    return pl.pallas_call(
        functools.partial(result_kernel, n_out),
        in_specs=[vmem] * 3 + [hbm] * 3,
        out_specs=[hbm, hbm],
        out_shape=[update, jax.ShapeDtypeStruct(c.shape, F32)],
        scratch_shapes=[
            pltpu.VMEM(update.shape, BF16),
            pltpu.VMEM(c.shape, F32),
            pltpu.VMEM(far.shape, BF16),
            pltpu.VMEM(grad_t.shape, BF16),
            pltpu.VMEM(c.shape, F32),
            pltpu.SemaphoreType.DMA((3,)),
            pltpu.SemaphoreType.DMA((3,)),
        ],
        compiler_params=pltpu.CompilerParams(vmem_limit_bytes=12 * MIB),
        name="result",
    )(tiles, inv, in_vmem(near), in_hbm(far), in_hbm(grad_t), in_hbm(c))


def spread(piece, count):
    return jnp.broadcast_to(piece[None], (count,) + piece.shape)


def grouped(n_in, n_out, key):
    groups = {}
    for i in range(n_in * n_out):
        inner, outer = divmod(i, n_out)
        x_lo, y = divmod(inner, n_in // 2)
        place = x_lo, y, outer // 4, outer // 2 % 2, outer % 2
        groups.setdefault(key(*place), []).append(i)
    return list(groups.values())


def exchange_groups(n_in, n_out):
    first = grouped(n_in, n_out, lambda x_lo, y, z, x_hi, core: (core, x_hi, y if core else z))
    second = grouped(n_in, n_out, lambda x_lo, y, z, x_hi, core: (core, x_lo, z if core else y))
    column = grouped(n_in, n_out, lambda x_lo, y, z, x_hi, core: (x_lo, x_hi, y))
    plane = grouped(n_in, n_out, lambda x_lo, y, z, x_hi, core: (z, core))
    return first, second, column, plane


def per_device(acts, grad_out, carried, start_seed):
    x, v, c = acts[0], grad_out[0], carried[0]
    n_in, n_out = lax.axis_size("inner"), lax.axis_size("outer")
    siblings = [(i, i ^ 1) for i in range(n_out)]
    both_axes = ("inner", "outer")
    first, second, column, plane = exchange_groups(n_in, n_out)

    keep, give, part = first_part(start_seed.reshape(1), v, c, x, n_in)
    with jax.named_scope("left_sum"):
        pair = (keep + lax.ppermute(give, "outer", siblings)).astype(BF16)
        got = lax.all_to_all(pair, both_axes, 0, 0, axis_index_groups=first)
        mine = jnp.sum(got.astype(F32), 0).astype(BF16)
        part, mine = lax.optimization_barrier((part, mine))
        got = lax.all_to_all(spread(mine, len(second[0])), both_axes, 0, 0, axis_index_groups=second)
        mine = jnp.sum(got.astype(F32), 0).astype(BF16)
    with jax.named_scope("grad"):
        grad_t = lax.psum_scatter(part.reshape(-1, part.shape[2]), "inner", scatter_dimension=0, tiled=True)
    with jax.named_scope("left_gather"):
        near = lax.all_to_all(spread(mine, len(first[0])), both_axes, 0, 0, axis_index_groups=first)
        far = lax.ppermute(near, "outer", siblings)
    tiles, inv = right_part(near, far, v, c, x)
    inv = factor(inv)
    with jax.named_scope("right_sum"):
        got = lax.all_to_all(tiles, both_axes, 0, 0, axis_index_groups=column)
        mine = jnp.sum(got.astype(F32), 0).astype(BF16)
        got = lax.all_to_all(spread(mine, len(plane[0])), both_axes, 0, 0, axis_index_groups=plane)
        mine = jnp.sum(got.astype(F32), 0).astype(BF16)
        tiles = lax.all_to_all(spread(mine, len(column[0])), both_axes, 0, 0, axis_index_groups=column)
    update_t, new_carried = result(tiles, inv, near, far, grad_t, c, n_out)
    return (update_t.T, new_carried[None])


def solution(mesh):
    placed = (P("outer", "inner", None), P("outer", "inner", None), P("outer", "inner", None), P())
    return jax.shard_map(
        per_device,
        mesh=mesh,
        in_specs=placed,
        out_specs=(P(None, "outer"), P("outer", "inner", None)),
        check_vma=False,
    )
```

```python
import functools

import jax
import jax.numpy as jnp
from jax import lax
from jax.experimental import pallas as pl
from jax.experimental.pallas import tpu as pltpu
from jax.sharding import PartitionSpec as P

RANK = 64
LANES = 128
HI = lax.Precision.HIGHEST
F32 = jnp.float32
BF16 = jnp.bfloat16
MIB = 1024 * 1024


def seeded_start_t(seed, width):
    shape = (RANK, width)
    index = lax.broadcasted_iota(jnp.int32, shape, 1) * RANK + lax.broadcasted_iota(jnp.int32, shape, 0)
    hashed = index * jnp.int32(73856093) ^ (seed * jnp.int32(19349663))
    hashed = hashed ^ lax.shift_right_logical(hashed, jnp.int32(13))
    hashed = hashed * jnp.int32(1274126177)
    hashed = hashed ^ lax.shift_right_logical(hashed, jnp.int32(16))
    return (hashed & jnp.int32(16777215)).astype(F32) / 16777216.0 - 0.5


def terms(a, count):
    out = []
    for _ in range(count):
        out.append(a.astype(BF16))
        a = a - out[-1].astype(F32)
    return out


def dot(a, b, dims, **kw):
    return lax.dot_general(a, b, (dims, ((), ())), preferred_element_type=F32, **kw)


NN = ((1,), (0,))
NT = ((1,), (1,))
TN = ((0,), (0,))


def factor_kernel(gram_ref, out_ref):
    *_, out_ref[...] = elimination(gram_ref[...])


def factor(gram):
    vmem = pl.BlockSpec(memory_space=pltpu.VMEM)
    return pl.pallas_call(
        factor_kernel,
        in_specs=[vmem],
        out_specs=vmem,
        out_shape=pltpu.VMEM((RANK, RANK), F32),
        compiler_params=pltpu.CompilerParams(vmem_limit_bytes=4 * MIB),
        cost_estimate=pl.CostEstimate(flops=4_000_000, bytes_accessed=2_000_000, transcendentals=0),
        name="factor",
    )(gram)


def position():
    outer = lax.axis_index("outer")
    return lax.axis_index("inner"), outer, lax.rem(outer, 2)


def in_hbm(a):
    return pltpu.with_memory_space_constraint(a, pltpu.HBM)


def in_vmem(a):
    return pltpu.with_memory_space_constraint(a, pltpu.VMEM)


def fetch(pairs, sems):
    copies = [pltpu.make_async_copy(a, b, sems.at[k]) for k, (a, b) in enumerate(pairs)]
    for copy in copies:
        copy.start()
    return copies


def first_kernel(seed_ref, v_hbm, c_hbm, x_hbm, keep_ref, give_ref, part_hbm, v_ref, c_ref, x_ref, part_ref, in_sems, out_sems):
    inner, _, core = position()
    count, tokens, wide = x_ref.shape
    blocks = [(x_hbm.at[:, pl.ds(j * wide, wide)], x_ref.at[j]) for j in range(count)]
    v_copy, c_copy, *x_copies = fetch([(v_hbm, v_ref), (c_hbm, c_ref)] + blocks, in_sems)
    start_t = seeded_start_t(seed_ref[0], v_ref.shape[1])
    start_3 = jnp.concatenate(terms(start_t, 3), 0)
    v_copy.wait()
    parts = dot(start_3, v_ref[...], NT)
    vs_t = parts[:RANK] + parts[RANK : 2 * RANK] + parts[2 * RANK :]
    v_t = v_ref[...].astype(F32).T.astype(BF16)
    lhs = jnp.concatenate(terms(vs_t, 2) + [v_t], 0)
    per = wide // (2 * LANES)
    out_copies = []
    for j in range(count):
        x_copies[j].wait()
        both = dot(lhs, x_ref[j], NN)
        left = both[:RANK] + both[RANK : 2 * RANK]
        for n in range(per):
            k = j * per + n
            cols = slice(2 * n * LANES, 2 * (n + 1) * LANES)
            block = left[:, cols]
            even, odd = block[:, :LANES], block[:, LANES:]
            keep_ref[k] = jnp.where(core == 0, even, odd)
            give_ref[k] = jnp.where(core == 0, odd, even)
            part_ref[k] = both[2 * RANK :, cols].astype(BF16)
        span = pl.ds(j * per, per)
        out_copies += fetch([(part_ref.at[span], part_hbm.at[span])], out_sems.at[pl.ds(j, 1)])
    c_copy.wait()
    c_2 = terms(c_ref[...], 2)
    cs = dot(start_3, c_2[0], NT) + dot(start_3, c_2[1], NT)
    cs = cs[:RANK] + cs[RANK : 2 * RANK] + cs[2 * RANK :]
    even, odd = cs[:, :LANES], cs[:, LANES:]
    keep_ref[inner] += jnp.where(core == 0, even, odd)
    give_ref[inner] += jnp.where(core == 0, odd, even)
    for copy in out_copies:
        copy.wait()


def first_part(seed, v, c, x, n_in):
    tokens, feats = x.shape
    width = v.shape[1]
    count = 4
    vmem, hbm = pl.BlockSpec(memory_space=pltpu.VMEM), pl.BlockSpec(memory_space=pltpu.HBM)
    out = pltpu.VMEM((n_in, RANK, LANES), F32)
    part = pltpu.HBM((n_in, width, 2 * LANES), BF16)
    return pl.pallas_call(
        first_kernel,
        in_specs=[pl.BlockSpec(memory_space=pltpu.SMEM), hbm, hbm, hbm],
        out_specs=[vmem, vmem, hbm],
        out_shape=[out, out, part],
        scratch_shapes=[
            pltpu.VMEM(v.shape, BF16),
            pltpu.VMEM(c.shape, F32),
            pltpu.VMEM((count, tokens, feats // count), BF16),
            pltpu.VMEM((n_in, width, 2 * LANES), BF16),
            pltpu.SemaphoreType.DMA((count + 2,)),
            pltpu.SemaphoreType.DMA((count,)),
        ],
        compiler_params=pltpu.CompilerParams(vmem_limit_bytes=16 * MIB),
        name="first_part",
    )(seed, in_hbm(v), in_hbm(c), in_hbm(x))


def in_order(core, near, far):
    first = core == 0
    near, far = near.astype(F32), far.astype(F32)
    return jnp.concatenate([jnp.where(first, near, far), jnp.where(first, far, near)], 1).astype(BF16)


def elimination(gram):
    shape = (RANK, 2 * RANK)
    eye = lax.broadcasted_iota(jnp.int32, shape, 0) == lax.broadcasted_iota(jnp.int32, shape, 1)
    aug = jnp.concatenate([gram, eye[:, :RANK].astype(F32)], 1)
    blocks = [aug[8 * k : 8 * k + 8] for k in range(RANK // 8)]
    tile = blocks[0].shape
    sub = lax.broadcasted_iota(jnp.int32, tile, 0)
    full = lambda a: jnp.broadcast_to(a, tile)
    for j in range(0, RANK, 2):
        at, s = divmod(j, 8)
        row_0, row_1 = full(blocks[at][s : s + 1]), full(blocks[at][s + 1 : s + 2])
        a, b = full(row_0[:, j : j + 1]), full(row_0[:, j + 1 : j + 2])
        c = full(row_1[:, j + 1 : j + 2])
        over_a = 1.0 / a
        ratio = b * over_a
        scaled_0 = row_0 * over_a
        scaled_1 = (row_1 - ratio * row_0) / (c - ratio * b)
        for k in range(at, len(blocks)):
            col_0 = full(blocks[k][:, j : j + 1])
            col_1 = full(blocks[k][:, j + 1 : j + 2]) - col_0 * ratio
            if k == at:
                col_0, col_1 = jnp.where(sub > s, col_0, 0.0), jnp.where(sub > s + 1, col_1, 0.0)
            blocks[k] = blocks[k] - col_0 * scaled_0 - col_1 * scaled_1
        yield None
    aug = jnp.concatenate(blocks, 0)
    pivots = jnp.sum(jnp.where(eye, aug, 0.0), 1, keepdims=True)
    yield aug[:, RANK:] * lax.rsqrt(pivots)


def right_kernel(near_ref, far_ref, x_ref, v_hbm, c_hbm, out_ref, inv_ref, v_ref, c_ref, sems):
    inner, _, core = position()
    copies = fetch([(v_hbm, v_ref), (c_hbm, c_ref)], sems)
    per = 2
    lefts = [
        jnp.concatenate([in_order(core, near_ref[k + n], far_ref[k + n]) for n in range(per)], 1)
        for k in range(0, near_ref.shape[0], per)
    ]
    gram = 0.0
    for left in lefts:
        gram += dot(left, left, NT)
    for copy in copies:
        copy.wait()
    y = 0.0
    for k, left in enumerate(lefts):
        y += dot(x_ref[:, 2 * k * per * LANES : 2 * (k + 1) * per * LANES], left, NT)
    y_2 = jnp.concatenate(terms(y.T, 2), 0)
    own = in_order(core, near_ref[inner], far_ref[inner])
    both = dot(y_2, v_ref[...], NN)
    m = both[:RANK] + both[RANK:]
    for term in terms(c_ref[...], 2):
        m += dot(own, term, NN)
    inv_ref[...] = gram
    high = out_ref.shape[1]
    across = m.shape[1] // LANES
    for k in range(out_ref.shape[0]):
        r, q = divmod(k, across)
        out_ref[k] = m[high * r : high * (r + 1), q * LANES : (q + 1) * LANES].astype(out_ref.dtype)


def right_part(near, far, v, c, x):
    high = 16
    tiles = RANK // high * (v.shape[1] // LANES)
    vmem, hbm = pl.BlockSpec(memory_space=pltpu.VMEM), pl.BlockSpec(memory_space=pltpu.HBM)
    return pl.pallas_call(
        right_kernel,
        in_specs=[vmem, vmem, vmem, hbm, hbm],
        out_specs=[vmem, vmem],
        out_shape=[jax.ShapeDtypeStruct((tiles, high, LANES), BF16), pltpu.VMEM((RANK, RANK), F32)],
        scratch_shapes=[pltpu.VMEM(v.shape, BF16), pltpu.VMEM(c.shape, F32), pltpu.SemaphoreType.DMA((2,))],
        compiler_params=pltpu.CompilerParams(vmem_limit_bytes=12 * MIB),
        name="right_part",
    )(in_vmem(near), in_vmem(far), x, in_hbm(v), in_hbm(c))


def result_kernel(n_out, tiles_ref, inv_ref, near_ref, far_hbm, grad_hbm, c_hbm, update_hbm, new_hbm, update_ref, new_ref, far_ref, grad_ref, c_ref, in_sems, out_sems):
    copies = fetch([(far_hbm, far_ref), (grad_hbm, grad_ref), (c_hbm, c_ref)], in_sems)
    inner, outer, core = position()
    high = tiles_ref.shape[1]
    across = tiles_ref.shape[0] * high // RANK
    m_t = jnp.concatenate(
        [jnp.concatenate([tiles_ref[r * across + q] for q in range(across)], 1) for r in range(RANK // high)], 0
    )
    inv = inv_ref[...]
    parts = dot(jnp.concatenate(terms(inv, 3), 0), m_t, NN)
    right_t = (parts[:RANK] + parts[RANK : 2 * RANK] + parts[2 * RANK :]) / n_out
    q = dot(inv, right_t, TN, precision=HI)
    q_2 = terms(q, 2)
    copies[0].wait()
    own = in_order(core, near_ref[inner], far_ref[inner])
    approx = dot(jnp.concatenate([own, own], 0), jnp.concatenate(q_2, 0), TN)
    copies[1].wait()
    copies[2].wait()
    new_ref[...] = grad_ref[...].astype(F32).T + c_ref[...] - approx
    rows = new_ref.shape[0] // 2
    out = [(new_ref.at[pl.ds(k * rows, rows)], new_hbm.at[pl.ds(k * rows, rows)]) for k in range(2)]
    out_copies = fetch(out, out_sems)
    cols = update_ref.shape[0]
    shape = (cols, q.shape[1])
    pick = lax.broadcasted_iota(jnp.int32, shape, 1) == outer * cols + lax.broadcasted_iota(jnp.int32, shape, 0)
    pick = pick.astype(BF16)
    q_mine = jnp.concatenate([dot(pick, term, NT).astype(BF16) for term in q_2], 0)
    for i in range(near_ref.shape[0]):
        both = dot(q_mine, in_order(core, near_ref[i], far_ref[i]), NN)
        update_ref[:, 2 * i * LANES : 2 * (i + 1) * LANES] = (both[:cols] + both[cols:]).astype(BF16)
    out_copies += fetch([(update_ref, update_hbm)], out_sems.at[pl.ds(2, 1)])
    for copy in out_copies:
        copy.wait()


def result(tiles, inv, near, far, grad_t, c, n_out):
    vmem, hbm = pl.BlockSpec(memory_space=pltpu.VMEM), pl.BlockSpec(memory_space=pltpu.HBM)
    update = jax.ShapeDtypeStruct((c.shape[1] // n_out, near.shape[0] * 2 * LANES), BF16)
    return pl.pallas_call(
        functools.partial(result_kernel, n_out),
        in_specs=[vmem] * 3 + [hbm] * 3,
        out_specs=[hbm, hbm],
        out_shape=[update, jax.ShapeDtypeStruct(c.shape, F32)],
        scratch_shapes=[
            pltpu.VMEM(update.shape, BF16),
            pltpu.VMEM(c.shape, F32),
            pltpu.VMEM(far.shape, BF16),
            pltpu.VMEM(grad_t.shape, BF16),
            pltpu.VMEM(c.shape, F32),
            pltpu.SemaphoreType.DMA((3,)),
            pltpu.SemaphoreType.DMA((3,)),
        ],
        compiler_params=pltpu.CompilerParams(vmem_limit_bytes=12 * MIB),
        name="result",
    )(tiles, inv, in_vmem(near), in_hbm(far), in_hbm(grad_t), in_hbm(c))


def spread(piece, count):
    return jnp.broadcast_to(piece[None], (count,) + piece.shape)


def grouped(n_in, n_out, key):
    groups = {}
    for i in range(n_in * n_out):
        inner, outer = divmod(i, n_out)
        x_lo, y = divmod(inner, n_in // 2)
        place = x_lo, y, outer // 4, outer // 2 % 2, outer % 2
        groups.setdefault(key(*place), []).append(i)
    return list(groups.values())


def exchange_groups(n_in, n_out):
    first = grouped(n_in, n_out, lambda x_lo, y, z, x_hi, core: (core, x_hi, y if core else z))
    second = grouped(n_in, n_out, lambda x_lo, y, z, x_hi, core: (core, x_lo, z if core else y))
    column = grouped(n_in, n_out, lambda x_lo, y, z, x_hi, core: (x_lo, x_hi, y))
    plane = grouped(n_in, n_out, lambda x_lo, y, z, x_hi, core: (z, core))
    return first, second, column, plane


def per_device(acts, grad_out, carried, start_seed):
    x, v, c = acts[0], grad_out[0], carried[0]
    n_in, n_out = lax.axis_size("inner"), lax.axis_size("outer")
    siblings = [(i, i ^ 1) for i in range(n_out)]
    both_axes = ("inner", "outer")
    first, second, column, plane = exchange_groups(n_in, n_out)

    keep, give, part = first_part(start_seed.reshape(1), v, c, x, n_in)
    with jax.named_scope("left_sum"):
        pair = (keep + lax.ppermute(give, "outer", siblings)).astype(BF16)
        got = lax.all_to_all(pair, both_axes, 0, 0, axis_index_groups=first)
        mine = jnp.sum(got.astype(F32), 0).astype(BF16)
        part, mine = lax.optimization_barrier((part, mine))
        got = lax.all_to_all(spread(mine, len(second[0])), both_axes, 0, 0, axis_index_groups=second)
        mine = jnp.sum(got.astype(F32), 0).astype(BF16)
    with jax.named_scope("grad"):
        grad_t = lax.psum_scatter(part.reshape(-1, part.shape[2]), "inner", scatter_dimension=0, tiled=True)
    with jax.named_scope("left_gather"):
        near = lax.all_to_all(spread(mine, len(first[0])), both_axes, 0, 0, axis_index_groups=first)
        far = lax.ppermute(near, "outer", siblings)
    tiles, inv = right_part(near, far, v, c, x)
    inv = factor(inv)
    with jax.named_scope("right_sum"):
        got = lax.all_to_all(tiles, both_axes, 0, 0, axis_index_groups=column)
        mine = jnp.sum(got.astype(F32), 0).astype(BF16)
        got = lax.all_to_all(spread(mine, len(plane[0])), both_axes, 0, 0, axis_index_groups=plane)
        mine = jnp.sum(got.astype(F32), 0).astype(BF16)
        inv, mine = lax.optimization_barrier((inv, mine))
        tiles = lax.all_to_all(spread(mine, len(column[0])), both_axes, 0, 0, axis_index_groups=column)
    update_t, new_carried = result(tiles, inv, near, far, grad_t, c, n_out)
    return (update_t.T, new_carried[None])


def solution(mesh):
    placed = (P("outer", "inner", None), P("outer", "inner", None), P("outer", "inner", None), P())
    return jax.shard_map(
        per_device,
        mesh=mesh,
        in_specs=placed,
        out_specs=(P(None, "outer"), P("outer", "inner", None)),
        check_vma=False,
    )
```
